32 devices in a mesh: gz: 2 (over core), row: 4 (over y, x), col: 4 (over z).
Axes of the slice: x: 2, y: 2, z: 4, core: 2. Of those that a mesh axis runs over, the one named last changes fastest.
Arguments:
- front_matrix: float32 [4096, 4096], P('row', 'col'), may hold values from -6 to 6
- l_panels: float32 [2, 8, 4, 512, 256], P('gz', None, 'row', 'col'), may hold values from -6 to 6
- l_map: int32 [2, 8, 4, 512], P('gz', None, 'row'), may hold values from 0 to 1024, as said below
- u_panels: float32 [2, 8, 4, 512, 256], P('gz', None, 'col', 'row'), may hold values from -0.375 to 0.375
- u_map: int32 [2, 8, 4, 512], P('gz', None, 'col'), may hold values from 0 to 1024, as said below
Outputs:
- updated_front: float32 [4096, 4096], P('row', 'col')
The draws below stay inside these ranges and needn't reach their ends.
Inputs may be any that keep to these rules, and one draw needn't show every extreme that they name: l_map[z,h,p,:] lists distinct rows of row block p updated by child h of layer z, used slots first, listed block of 128 rows by block, at most 64 rows to a block; unused slots hold 1024; in every child some row block uses all 512 slots. u_map[z,h,q,:] lists distinct columns of column block q updated by child h of layer z, used slots first, listed block of 128 columns by block, at most 64 to a block; unused slots hold 1024; in every child some column block uses all 512 slots.
All inputs are finite; a program needn't handle non-finite values.
Results may differ from the reference program's by a relative error of at most 0.0001.
Values sent between devices are 32-bit elements; how exact they have to be, the bound alone decides.
No kernel may reach another device: no remote copies, remote signals or barrier semaphores. Data moves between devices by JAX's collectives and lax.ppermute only.
A program may use at most 64 MiB of HBM per device.

```python
import jax
import jax.numpy as jnp
from jax import lax

F = 4096
K = 256
TILE = 128
HT = 64
NCH = 8
NL = 2
FT = 32
FR = 1024
FC = 1024
TPR = 8
TPC = 8
RL = 512
RU = 512
N_ROW = 4
N_COL = 4


def index_sets(key):
    key_counts, key_rowfull, key_colfull, key_places = jax.random.split(key, 4)
    counts = jax.random.randint(key_counts, (NL, NCH, FT), HT // 4, HT + 1)
    full_row = jax.random.randint(key_rowfull, (NL, NCH, 1), 0, FT // TPR)
    full_col = jax.random.randint(key_colfull, (NL, NCH, 1), 0, FT // TPC)
    tile_ids = jnp.arange(FT, dtype=jnp.int32)[None, None, :]
    forced = (tile_ids // TPR == full_row) | (tile_ids // TPC == full_col)
    counts = jnp.where(forced, HT, counts)
    subkeys = jax.random.split(key_places, NL * NCH * FT)
    positions = jax.vmap(lambda single: jax.random.permutation(single, TILE))(subkeys)
    positions = positions.reshape(NL, NCH, FT, TILE).astype(jnp.int32)
    is_used = jnp.arange(TILE, dtype=jnp.int32)[None, None, None, :] < counts[..., None]
    return (positions, is_used)


def compact(positions, is_used, per_group, slots, width):
    group_count = FT // per_group
    span = per_group * TILE
    within = positions.reshape(NL, NCH, group_count, span)
    within = within + jnp.arange(span, dtype=jnp.int32) // TILE * TILE
    used = is_used.reshape(NL, NCH, group_count, span)
    slot_ids = jnp.arange(span, dtype=jnp.int32)
    ranked = jnp.where(used, slot_ids, slot_ids + span)
    ranking = jnp.argsort(ranked, axis=-1)[..., :slots]
    picked = jnp.take_along_axis(within, ranking, axis=-1)
    kept = jnp.take_along_axis(used, ranking, axis=-1)
    return jnp.where(kept, picked, width).astype(jnp.int32)


def draw_l_map(key, part):
    positions, is_used = index_sets(jax.random.fold_in(key, 11))
    return compact(positions, is_used, TPR, RL, FR)


def draw_u_map(key, part):
    positions, is_used = index_sets(jax.random.fold_in(key, 12))
    return compact(positions, is_used, TPC, RU, FC)


def block_scale(key, dims, shards, smallest, high):
    def one(axis_at, blocks):
        steps = jax.random.uniform(jax.random.fold_in(jax.random.fold_in(key, 6), axis_at), (blocks,), jnp.float32, smallest / len(shards), high / len(shards))
        return jnp.repeat(jnp.exp(steps), dims[axis_at] // blocks).reshape((-1,) + (1,) * (len(dims) - axis_at - 1))

    factor_of = one(*shards[0])
    for cut in shards[1:]:
        factor_of = factor_of * one(*cut)
    return factor_of


def centred(own_key, extent, scale, limit, shards=(), held_as=jnp.bfloat16):
    drawn = scale * jax.random.normal(own_key, extent, jnp.float32)
    if shards:
        drawn = drawn * block_scale(own_key, extent, shards, -0.22, 0.18)
    return jnp.clip(drawn, -limit, limit).astype(held_as)


def setup_inputs(seed: int = 0) -> dict:
    key_list = jax.random.split(jax.random.key(seed), 6)
    front_matrix = centred(key_list[0], (F, F), 1.0, 6.0, ((0, 4), (1, 4)), jnp.float32)
    l_panels = centred(key_list[1], (NL, NCH, N_ROW, RL, K), 1.0, 6.0, ((0, 2), (2, 4), (3, 4)), jnp.float32)
    l_map = draw_l_map(jax.random.fold_in(key_list[5], 71), 0)
    u_panels = centred(key_list[3], (NL, NCH, N_COL, RU, K), K ** -0.5, 0.375, ((0, 2), (2, 4), (3, 4)), jnp.float32)
    u_map = draw_u_map(jax.random.fold_in(key_list[5], 71), 0)
    return {"front_matrix": front_matrix, "l_panels": l_panels, "l_map": l_map, "u_panels": u_panels, "u_map": u_map}


def reference(front_matrix, l_panels, l_map, u_panels, u_map):
    update = jnp.zeros((F, F), jnp.float32)
    for layer_idx in range(NL):
        for child_idx in range(NCH):
            row_map = l_map[layer_idx, child_idx]
            col_map = u_map[layer_idx, child_idx]
            row_base = jnp.arange(N_ROW, dtype=jnp.int32)[:, None] * FR
            col_base = jnp.arange(N_COL, dtype=jnp.int32)[:, None] * FC
            row_index = jnp.where(row_map < FR, row_base + row_map, F).reshape(-1)
            col_index = jnp.where(col_map < FC, col_base + col_map, F).reshape(-1)
            left_panel = l_panels[layer_idx, child_idx].reshape(N_ROW * RL, K)
            right_panel = u_panels[layer_idx, child_idx].reshape(N_COL * RU, K)
            products = jnp.dot(left_panel, right_panel.T, precision=lax.Precision.HIGHEST, preferred_element_type=jnp.float32)
            update = update.at[row_index[:, None], col_index[None, :]].add(products, mode="drop")
    return front_matrix - update
```

```python
import functools

import jax
import jax.numpy as jnp
from jax import lax
from jax.experimental import pallas as pl
from jax.experimental.pallas import tpu as pltpu
from jax.sharding import PartitionSpec as P

F32 = jnp.float32
BF16 = jnp.bfloat16
VMEM_LIMIT = 48 * 1024 * 1024


def spread_dense(row_panel, row_map, col_dense, row_count):
    targets = jnp.arange(row_count, dtype=jnp.int32)
    narrow = jnp.einsum("hik,hgk->hig", row_panel, col_dense, precision=lax.Precision.HIGHEST)
    row_hot = (row_map[:, :, None] == targets[None, None, :]).astype(jnp.float32)
    return jnp.einsum("hif,hig->fg", row_hot, narrow, precision=lax.Precision.HIGHEST)


def any_mesh(front_matrix, l_panels, l_map, u_panels, u_map):
    row_count, col_count = front_matrix.shape
    row_map = l_map[0, :, 0, :]
    col_map = u_map[0, :, 0, :]
    col_panel = lax.all_gather(u_panels, "row", axis=3, tiled=True)[0, :, 0]
    col_targets = jnp.arange(col_count, dtype=jnp.int32)
    col_hot = (col_map[:, :, None] == col_targets[None, None, :]).astype(jnp.float32)
    col_dense = jnp.einsum("hjg,hjk->hgk", col_hot, col_panel, precision=lax.Precision.HIGHEST)
    row_panel = lax.all_gather(l_panels, "col", axis=3, tiled=True)[0, :, 0]
    update = spread_dense(row_panel, row_map, col_dense, row_count)
    summed = lax.psum(update, "gz")
    return front_matrix - summed


def split(x):
    high = x.astype(BF16)
    return high, (x - high.astype(F32)).astype(BF16)


def dot(a, b):
    return jnp.dot(a, b, preferred_element_type=F32)


def dot_t(a, b):
    return lax.dot_general(a, b, (((1,), (1,)), ((), ())), preferred_element_type=F32)


def one_hot(slots, first, count):
    rows = lax.broadcasted_iota(jnp.int32, (count, slots.shape[-1]), 0) + first
    return jnp.where(rows == slots, 1.0, 0.0).astype(BF16)


def densify_kernel(map_ref, own, by_x, by_y, by_xy_a, by_xy_b, high_ref, low_ref):
    here = lax.axis_index("row")
    child = pl.program_id(0)
    far = jnp.where(child < pl.num_programs(0) // 2, by_xy_a[0], by_xy_b[0])
    panel = jnp.concatenate([own[0], by_x[0], by_y[0], far], axis=0)
    count = high_ref.shape[1]
    hot = jnp.concatenate(
        [one_hot(map_ref[0, pl.ds(here ^ part, 1), :], 0, count) for part in range(4)], axis=1
    )
    high, low = split(panel)
    high_ref[0] = dot(hot, high).astype(BF16)
    low_ref[0] = dot(hot, low).astype(BF16)


def densify(col_map, own, by_x, by_y, by_xy_a, by_xy_b, col_count):
    children, part, depth = own.shape
    half = children // 2
    block = (1, part, depth)
    whole = pl.BlockSpec(block, lambda h: (h, 0, 0))
    dense = jax.ShapeDtypeStruct((children, col_count, depth), BF16)
    dense_spec = pl.BlockSpec((1, col_count, depth), lambda h: (h, 0, 0))
    return pl.pallas_call(
        densify_kernel,
        grid=(children,),
        in_specs=[
            pl.BlockSpec((1,) + col_map.shape[1:], lambda h: (h, 0, 0)),
            whole,
            whole,
            whole,
            pl.BlockSpec(block, lambda h: (jnp.minimum(h, half - 1), 0, 0)),
            pl.BlockSpec(block, lambda h: (jnp.maximum(h - half, 0), 0, 0)),
        ],
        out_specs=[dense_spec, dense_spec],
        out_shape=[dense, dense],
        compiler_params=pltpu.CompilerParams(vmem_limit_bytes=VMEM_LIMIT),
        cost_estimate=pl.CostEstimate(
            flops=4 * children * 4 * part * col_count * depth,
            bytes_accessed=children * depth * (16 * part + 4 * col_count),
            transcendentals=0,
        ),
    )(col_map, own, by_x, by_y, by_xy_a, by_xy_b)


def chunk_ids(here):
    end = (here == 0) | (here == 3)
    low = here < 2
    return here, here ^ 1, jnp.where(low, 2, 1), jnp.where(low, 3, 0)


def update_kernel(map_ref, own, pair, mid_a, mid_b, far_a, far_b, uh, ul, out_ref, lh, ll, hot, nh, nl):
    ids = chunk_ids(lax.axis_index("col"))
    children, part, depth = own.shape
    chunks = len(ids)
    rows = out_ref.shape[0]
    step = rows // chunks

    @pl.when(pl.program_id(0) == 0)
    def _():
        def prepare(h, carry):
            at = pl.ds(pl.multiple_of(h * part, part), part)
            panels = (own[h], pair[h], mid_a[h] + mid_b[h], far_a[h] + far_b[h])
            for c in range(chunks):
                high, low = split(panels[c])
                lh[h, c * part : (c + 1) * part, :] = high
                ll[h, c * part : (c + 1) * part, :] = low
                hot[c, :, at] = one_hot(map_ref[h, pl.ds(ids[c], 1), :], 0, rows)
            return carry

        lax.fori_loop(0, children, prepare, 0)

    def narrow(h, carry):
        at = pl.ds(pl.multiple_of(h * part, part), part)
        n = dot_t(lh[h], uh[h]) + dot_t(lh[h], ul[h]) + dot_t(ll[h], uh[h])
        high, low = split(n)
        for c in range(chunks):
            nh[c, at, :] = high[c * part : (c + 1) * part]
            nl[c, at, :] = low[c * part : (c + 1) * part]
        return carry

    lax.fori_loop(0, children, narrow, 0)
    out_ref[...] = jnp.zeros_like(out_ref)
    for c in range(chunks):

        def place(j, carry, c=c):
            at = pl.ds(pl.multiple_of(j * step, step), step)
            a = hot[c, at, :]
            out_ref[at, :] += dot(a, nh[c]) + dot(a, nl[c])
            return carry

        lax.fori_loop(ids[c], chunks, place, 0)


def update_of(row_map, panels, dense, row_count):
    own = panels[0]
    children, part, depth = own.shape
    col_count = dense[0].shape[1]
    wide = 256
    chunks = 4
    whole = pl.BlockSpec(own.shape, lambda g: (0, 0, 0))
    dense_spec = pl.BlockSpec((children, wide, depth), lambda g: (0, g, 0))
    slots = children * part
    return pl.pallas_call(
        update_kernel,
        grid=(col_count // wide,),
        in_specs=[pl.BlockSpec(row_map.shape, lambda g: (0, 0, 0))] + [whole] * 6 + [dense_spec] * 2,
        out_specs=pl.BlockSpec((row_count, wide), lambda g: (0, g)),
        out_shape=jax.ShapeDtypeStruct((row_count, col_count), F32),
        scratch_shapes=[
            pltpu.VMEM((children, chunks * part, depth), BF16),
            pltpu.VMEM((children, chunks * part, depth), BF16),
            pltpu.VMEM((chunks, row_count, slots), BF16),
            pltpu.VMEM((chunks, slots, wide), BF16),
            pltpu.VMEM((chunks, slots, wide), BF16),
        ],
        compiler_params=pltpu.CompilerParams(vmem_limit_bytes=VMEM_LIMIT),
        cost_estimate=pl.CostEstimate(
            flops=6 * chunks * slots * col_count * depth + 3 * chunks * slots * row_count * col_count,
            bytes_accessed=4 * row_count * col_count + 4 * children * col_count * depth,
            transcendentals=0,
        ),
    )(row_map, *panels, *dense)


ENDS = [(0, 1), (1, 0), (2, 3), (3, 2)]
MIDDLE = [(1, 2), (2, 1)]
OUTWARD = [(1, 0), (2, 3)]
SWAP_X = [(0, 1), (1, 0), (2, 3), (3, 2)]
SWAP_Y = [(0, 2), (2, 0), (1, 3), (3, 1)]


def four_by_four(front_matrix, l_panels, l_map, u_panels, u_map):
    row_count, col_count = front_matrix.shape
    l_own = l_panels[0, :, 0]
    u_own = u_panels[0, :, 0]
    half = u_own.shape[0] // 2
    row_map = l_map.reshape(l_own.shape[0], 4, -1)
    col_map = u_map.reshape(u_own.shape[0], 4, -1)
    pair = lax.ppermute(l_own, "col", ENDS)
    mid_b = lax.ppermute(l_own, "col", MIDDLE)
    by_x = lax.ppermute(u_own, "row", SWAP_X)
    by_y = lax.ppermute(u_own, "row", SWAP_Y)
    mid_a = lax.ppermute(mid_b, "col", OUTWARD)
    far_b = lax.ppermute(pair, "col", MIDDLE)
    far_a = lax.ppermute(far_b, "col", OUTWARD)
    by_xy_a = lax.ppermute(by_x[:half], "row", SWAP_Y)
    by_xy_b = lax.ppermute(by_y[half:], "row", SWAP_X)
    dense = densify(col_map, u_own, by_x, by_y, by_xy_a, by_xy_b, col_count)
    mine = update_of(row_map, (l_own, pair, mid_a, mid_b, far_a, far_b), dense, row_count)
    other = lax.ppermute(mine, "gz", [(0, 1), (1, 0)])
    return front_matrix - (mine + other)


def solution(mesh):
    placed = (
        P("row", "col"),
        P("gz", None, "row", "col", None),
        P("gz", None, "row", None),
        P("gz", None, "col", "row", None),
        P("gz", None, "col", None),
    )
    square = mesh.shape["row"] == 4 and mesh.shape["col"] == 4
    return jax.shard_map(
        four_by_four if square else any_mesh,
        mesh=mesh,
        in_specs=placed,
        out_specs=P("row", "col"),
        check_vma=False,
    )
```

```python
import functools

import jax
import jax.numpy as jnp
from jax import lax
from jax.experimental import pallas as pl
from jax.experimental.pallas import tpu as pltpu
from jax.sharding import PartitionSpec as P

F32 = jnp.float32
BF16 = jnp.bfloat16
VMEM_ALL = 60 * 1024 * 1024


def spread_dense(row_panel, row_map, col_dense, row_count):
    targets = jnp.arange(row_count, dtype=jnp.int32)
    narrow = jnp.einsum("hik,hgk->hig", row_panel, col_dense, precision=lax.Precision.HIGHEST)
    row_hot = (row_map[:, :, None] == targets[None, None, :]).astype(jnp.float32)
    return jnp.einsum("hif,hig->fg", row_hot, narrow, precision=lax.Precision.HIGHEST)


def any_mesh(front_matrix, l_panels, l_map, u_panels, u_map):
    row_count, col_count = front_matrix.shape
    row_map = l_map[0, :, 0, :]
    col_map = u_map[0, :, 0, :]
    col_panel = lax.all_gather(u_panels, "row", axis=3, tiled=True)[0, :, 0]
    col_targets = jnp.arange(col_count, dtype=jnp.int32)
    col_hot = (col_map[:, :, None] == col_targets[None, None, :]).astype(jnp.float32)
    col_dense = jnp.einsum("hjg,hjk->hgk", col_hot, col_panel, precision=lax.Precision.HIGHEST)
    row_panel = lax.all_gather(l_panels, "col", axis=3, tiled=True)[0, :, 0]
    update = spread_dense(row_panel, row_map, col_dense, row_count)
    summed = lax.psum(update, "gz")
    return front_matrix - summed


def split(x):
    high = x.astype(BF16)
    return high, (x - high.astype(F32)).astype(BF16)


def dot(a, b):
    return jnp.dot(a, b, preferred_element_type=F32)


def dot_t(a, b):
    return lax.dot_general(a, b, (((1,), (1,)), ((), ())), preferred_element_type=F32)


def one_hot(slots, first, count):
    rows = lax.broadcasted_iota(jnp.int32, (count, slots.shape[-1]), 0) + first
    return jnp.where(rows == slots, 1.0, 0.0).astype(BF16)


def chunk_ids(here):
    low = here < 2
    return here, here ^ 1, jnp.where(low, 2, 1), jnp.where(low, 3, 0)


def dense_columns(slots, panel_ref, count):
    half = panel_ref.shape[0] // 2
    top = dot(one_hot(slots[:, :half], 0, count // 2), panel_ref[:half, :])
    return jnp.concatenate([top, dot(one_hot(slots, count // 2, count // 2), panel_ref[...])], axis=0)


def stage_kernel(plan, *refs):
    n_in, n_out = plan["inputs"], plan["outputs"]
    bases = [[refs[i] for i in pieces] for pieces in plan["bases"]]
    hbm_in, hbm_out = refs[:n_in], refs[n_in : n_in + n_out]
    scratch = refs[n_in + n_out :]
    held = dict(zip(plan["held"], scratch))
    acc, slots_ref, high_ref, low_ref = scratch[len(held) : len(held) + 4]
    n_staged = 2 * plan["emit"] + plan["sums"]
    staged = scratch[len(held) + 4 : len(held) + 4 + n_staged]
    extra = scratch[len(held) + 4 + n_staged : -4]
    panel_ref = scratch[-4]
    in_sem, base_sem, out_sem = scratch[-3:]
    ids = chunk_ids(lax.axis_index("col"))
    here = lax.axis_index("row")
    layer = lax.axis_index("gz")
    row_count, cols = acc.shape
    part, rows = plan["part"], plan["rows"]
    blocks = row_count // rows
    first_dense = n_out - n_staged

    def offset(first):
        return first(layer) if callable(first) else first

    def whole(i):
        lane = plan["held"].index(i)
        first, count = plan["range"][i]
        return pltpu.make_async_copy(hbm_in[i].at[pl.ds(first, count)], held[i], in_sem.at[lane, 0])

    def one(i, child):
        lane = plan["held"].index(i)
        first, _ = plan["range"][i]
        return pltpu.make_async_copy(hbm_in[i].at[first + child], held[i].at[child], in_sem.at[lane, child])

    def base_copy(n, block, piece=0, at_piece=0):
        at = pl.ds(pl.multiple_of(block * rows, rows), rows)
        target = acc if n == 0 else extra[n - 1]
        source = bases[n][piece].at[pl.ds(at_piece * rows, rows)]
        return pltpu.make_async_copy(source, target.at[at], base_sem.at[n, block])

    def dense_copy(n, child):
        return pltpu.make_async_copy(
            staged[n].at[child], hbm_out[first_dense + n].at[child], out_sem.at[1 + n, child]
        )

    each = blocks // plan["pieces"]

    def out_copy(block, piece):
        at = pl.ds(pl.multiple_of(block * rows, rows), rows)
        to = pl.ds(pl.multiple_of((block - piece * each) * rows, rows), rows)
        return pltpu.make_async_copy(acc.at[at], hbm_out[piece].at[to], out_sem.at[0, block])

    for i in plan["held"]:
        if i not in plan["single"]:
            whole(i).start()
    for group in plan["groups"]:
        for child in range(group["count"]):
            for i in group["dense"]:
                one(i, child).start()
    for block in range(blocks):
        for n, pieces in enumerate(bases):
            per = blocks // len(pieces)
            base_copy(n, block, block // per, block % per).start()
    for i in plan["held"]:
        if i not in plan["single"]:
            whole(i).wait()

    for group in plan["groups"]:

        def narrow(child, carry, group=group):
            if "u" in group:
                panels = [held[i][child] for i in group["u"][:3]]
                far_a, far_b = (held[i] for i in group["u"][3:])
                cut = group["cut"]
                in_a = far_a[jnp.minimum(child, cut - 1)]
                in_b = far_b[jnp.maximum(child - cut, 0)]
                panels.append(jnp.where(child < cut, in_a, in_b))
                for number, x in enumerate(panels):
                    high, low = split(x)
                    at = pl.ds(pl.multiple_of((here ^ number) * part, part), part)
                    panel_ref[at, :] = jnp.concatenate([high, low], axis=1)
                full = dense_columns(held[group["col_map"]][child], panel_ref, cols)
                depth = full.shape[1] // 2
                full_high, full_low = full[:, :depth], full[:, depth:]
                dense_high, dense_low = full_high.astype(BF16), full_low.astype(BF16)
                staged[0][child] = dense_high
                staged[1][child] = dense_low
                for n in range(2):
                    dense_copy(n, child).start()

                for c in range(plan["sums"]):

                    @pl.when(child == c)
                    def _(c=c):
                        staged[2 + c][0] = full_high + full_low
                        dense_copy(2 + c, 0).start()

            else:
                for i in group["dense"]:
                    one(i, child).wait()
                if len(group["dense"]) == 2:
                    dense_high, dense_low = (held[i][child] for i in group["dense"])
                else:
                    dense_high, dense_low = split(held[group["dense"][0]][child])
            panels = []
            for place, first, which, members in group["chunks"]:
                panels.append(sum(held[m][child] for m in members))
                at = pl.ds(pl.multiple_of((child + offset(first)) * part, part), part)
                slots_ref[place, :, at] = held[group["map"]][child, pl.ds(ids[which], 1), :]
            high, low = split(jnp.concatenate(panels, axis=0))
            both = dot_t(jnp.concatenate([high, low], axis=0), dense_high)
            count = high.shape[0]
            n_high, n_low = split(both[:count] + both[count:] + dot_t(high, dense_low))
            for number, (place, first, _, _) in enumerate(group["chunks"]):
                cut = slice(number * part, (number + 1) * part)
                at = pl.ds(pl.multiple_of((child + offset(first)) * part, part), part)
                high_ref[place, at, :] = n_high[cut]
                low_ref[place, at, :] = n_low[cut]
            return carry

        lax.fori_loop(0, group["count"], narrow, 0)

    def finish(block, carry):
        at = pl.ds(pl.multiple_of(block * rows, rows), rows)
        if bases:
            for n in range(len(bases)):
                base_copy(n, block).wait()
            if plan["one_layer"]:
                acc[at, :] = jnp.where(layer == 0, acc[at, :], 0.0)
            if len(bases) > 1:
                acc[at, :] += sum(e[at, :] for e in extra)
        else:
            acc[at, :] = jnp.zeros((rows, cols), F32)
        for place, (which, count) in enumerate(plan["places"]):
            used = count * part

            @pl.when(ids[which] <= block)
            def _(place=place, used=used):
                hot = one_hot(slots_ref[place, :, :used], block * rows, rows)
                acc[at, :] -= dot(hot, high_ref[place, :used]) + dot(hot, low_ref[place, :used])

        for piece in range(plan["pieces"]):

            @pl.when((block >= piece * each) & (block < (piece + 1) * each))
            def _(piece=piece):
                out_copy(block, piece).start()

        return carry

    lax.fori_loop(0, blocks, finish, 0)
    for block in range(blocks):
        out_copy(block, block // each).wait()
    for n in range(n_staged):
        for child in range(plan["groups"][0]["count"] if n < 2 else 1):
            dense_copy(n, child).wait()


def stage(shape, bases, places, groups, emit_sums=None, pieces=1, one_layer=False):
    row_count, col_count = shape
    inputs, base_at = [], []
    for base in bases:
        base_at.append(list(range(len(inputs), len(inputs) + len(base))))
        inputs += base
    held, ranges, single, layout = [], {}, [], []

    def take(pair, count):
        array, first = pair
        low, high = max(first, 0), min(first + count, array.shape[0])
        if high <= low:
            low, high = 0, 1
        inputs.append(array)
        held.append(len(inputs) - 1)
        ranges[held[-1]] = (low, high - low)
        return held[-1]

    for g in groups:
        count = g["count"]
        item = dict(count=count, map=take(g["map"], count), dense=[])
        if "u" in g:
            item["col_map"] = take(g["col_map"], count)
            item["u"] = [take(p, count) for p in g["u"]]
            item["cut"] = g["cut"]
        else:
            item["dense"] = [take(p, count) for p in g["dense"]]
            single += item["dense"]
        item["chunks"] = [
            (place, first, places[place][0], [take(p, count) for p in panels])
            for place, first, panels in g["chunks"]
        ]
        part, depth = g["chunks"][0][2][0][0].shape[1:]
        layout.append(item)
    rows = 2 * part
    most = max(count for _, count in places)
    total = groups[0]["count"]
    out_shape = [jax.ShapeDtypeStruct((row_count // pieces, col_count), F32)] * pieces
    emit = emit_sums is not None
    sums = emit_sums or 0
    dense_shapes = [((total, col_count, depth), BF16)] * (2 * emit) + [((1, col_count, depth), F32)] * sums
    out_shape += [jax.ShapeDtypeStruct(*x) for x in dense_shapes]
    plan = dict(
        inputs=len(inputs),
        outputs=len(out_shape),
        bases=base_at,
        pieces=pieces,
        held=held,
        range=ranges,
        single=single,
        groups=layout,
        places=places,
        emit=emit,
        sums=sums,
        one_layer=one_layer,
        part=part,
        rows=rows,
    )
    deepest = max(g["count"] for g in groups)
    blocks = row_count // rows
    kept = set(single)
    buffers = (
        [((ranges[i][1],) + inputs[i].shape[1:], inputs[i].dtype) for i in held]
        + [
            (shape, F32),
            ((len(places), 1, most * part), jnp.int32),
            ((len(places), most * part, col_count), BF16),
            ((len(places), most * part, col_count), BF16),
        ]
        + dense_shapes
        + [(shape, F32)] * max(len(bases) - 1, 0)
        + [((4 * part, 2 * depth), BF16)]
    )
    return pl.pallas_call(
        functools.partial(stage_kernel, plan),
        in_specs=[pl.BlockSpec(memory_space=pl.ANY if i in kept else pltpu.HBM) for i in range(len(inputs))],
        out_specs=[pl.BlockSpec(memory_space=pltpu.HBM)] * pieces + [pl.BlockSpec(memory_space=pl.ANY)] * len(dense_shapes),
        out_shape=out_shape,
        scratch_shapes=[pltpu.VMEM(dims, kind) for dims, kind in buffers]
        + [
            pltpu.SemaphoreType.DMA((len(held), deepest)),
            pltpu.SemaphoreType.DMA((max(len(bases), 1), blocks)),
            pltpu.SemaphoreType.DMA((1 + len(dense_shapes), max(blocks, total))),
        ],
        compiler_params=pltpu.CompilerParams(vmem_limit_bytes=VMEM_ALL),
        cost_estimate=pl.CostEstimate(flops=1000, bytes_accessed=1000, transcendentals=0),
    )(*inputs)


ENDS = [(0, 1), (1, 0), (2, 3), (3, 2)]
MIDDLE = [(1, 2), (2, 1)]
OUTWARD = [(1, 0), (2, 3)]
SWAP_X = [(0, 1), (1, 0), (2, 3), (3, 2)]
SWAP_Y = [(0, 2), (2, 0), (1, 3), (3, 1)]
SWAP_XY = [(0, 3), (3, 0), (1, 2), (2, 1)]


def four_by_four(front_matrix, l_panels, l_map, u_panels, u_map):
    shape = front_matrix.shape
    l_own = l_panels[0, :, 0]
    u_own = u_panels[0, :, 0]
    children = u_own.shape[0]
    first = children // 2
    late = children * 3 // 8
    rest, early = children - first, children - late
    row_map = l_map.reshape(children, 4, -1)
    col_map = u_map.reshape(children, 1, -1)
    swap = [(0, 1), (1, 0)]
    together = lax.optimization_barrier

    quarter = first // 2
    pair = lax.ppermute(l_own, "col", ENDS)
    mid_b = lax.ppermute(l_own, "col", MIDDLE)
    by_x = lax.ppermute(u_own, "row", SWAP_X)
    by_y = lax.ppermute(u_own, "row", SWAP_Y)
    pair, mid_b, by_x, by_y = together((pair, mid_b, by_x, by_y))

    def diagonal(start):
        cut = start + quarter
        return (
            lax.ppermute(by_x[start:cut], "row", SWAP_Y),
            lax.ppermute(by_y[cut : start + first], "row", SWAP_X),
        )

    by_xy1 = diagonal(0)
    far_b = lax.ppermute(pair, "col", MIDDLE)
    mid_a = lax.ppermute(mid_b, "col", OUTWARD)
    by_xy2 = diagonal(first)
    row_map_other = lax.ppermute(row_map, "gz", swap)

    def near(base, start, u, chunks=(), groups=(), **options):
        group = dict(
            count=first,
            map=(row_map, start),
            col_map=(col_map, start),
            u=[(u_own, start), (by_x, start), (by_y, start)] + [(x, 0) for x in u],
            cut=quarter,
            chunks=[(0, 0, [(l_own, start)]), (1, 0, [(pair, start)]), *chunks],
        )
        places = [(0, first), (1, first)] + [(2, children)] * len(chunks)
        return stage(shape, [base], places, [group, *groups], **options)

    mine, *dense1 = near([front_matrix], 0, by_xy1, emit_sums=late, one_layer=True)
    dense1, sums = dense1[:2], dense1[2:]
    far_b, mine = together((far_b, mine))
    far_b2, far_b1 = far_b[:late], far_b[late:]
    far_a1 = lax.ppermute(far_b1, "col", OUTWARD)
    far_a2 = lax.ppermute(far_b2, "col", OUTWARD)
    far_b2_other = lax.ppermute(far_b2, "gz", swap)
    *sums, by_xy2a, by_xy2b = together((*sums, *by_xy2))
    sums_other = [lax.ppermute(x, "gz", swap) for x in sums]
    mine, *dense2 = near(
        [mine],
        first,
        (by_xy2a, by_xy2b),
        [(2, first, [(mid_a, first), (mid_b, first)])],
        [
            dict(
                count=first,
                map=(row_map, 0),
                dense=[(d, 0) for d in dense1],
                chunks=[(2, 0, [(mid_a, 0), (mid_b, 0)])],
            )
        ],
        emit_sums=0,
    )
    mine, far_b2_other, *sums_other = together((mine, far_b2_other, *sums_other))
    top, bottom = stage(
        shape,
        [[mine]],
        [(3, early)],
        [
            dict(
                count=first - late,
                map=(row_map, late),
                dense=[(d, late) for d in dense1],
                chunks=[(0, 0, [(far_a1, 0), (far_b1, 0)])],
            ),
            dict(
                count=rest,
                map=(row_map, first),
                dense=[(d, 0) for d in dense2],
                chunks=[(0, first - late, [(far_a1, first - late), (far_b1, first - late)])],
            ),
        ],
        pieces=2,
    )
    other_top = lax.ppermute(top, "gz", swap)
    sent, far_a2 = together((bottom, far_a2))
    far_a2_other = lax.ppermute(far_a2, "gz", swap)
    other_bottom = lax.ppermute(sent, "gz", swap)
    late_groups = [
        dict(
            count=1,
            map=(slot_map, c),
            dense=[(x, 0)],
            chunks=[(0, at, [(far, c) for far in fars])],
        )
        for slot_map, denses, fars, at in (
            (row_map, sums, (far_a2, far_b2), lambda layer: layer * late),
            (row_map_other, sums_other, (far_a2_other, far_b2_other), lambda layer: (1 - layer) * late),
        )
        for c, x in enumerate(denses)
    ]
    for g in late_groups:
        place, at, fars = g["chunks"][0]
        g["chunks"] = [(place, functools.partial(lambda at, c, layer: at(layer) + c, at, g["map"][1]), fars)]
    (out,) = stage(shape, [[top, bottom], [other_top, other_bottom]], [(3, 2 * late)], late_groups)
    return out


def solution(mesh):
    placed = (
        P("row", "col"),
        P("gz", None, "row", "col", None),
        P("gz", None, "row", None),
        P("gz", None, "col", "row", None),
        P("gz", None, "col", None),
    )
    square = mesh.shape["row"] == 4 and mesh.shape["col"] == 4
    return jax.shard_map(
        four_by_four if square else any_mesh,
        mesh=mesh,
        in_specs=placed,
        out_specs=P("row", "col"),
        check_vma=False,
    )
```

```python
import functools

import jax
import jax.numpy as jnp
from jax import lax
from jax.experimental import pallas as pl
from jax.experimental.pallas import tpu as pltpu
from jax.sharding import PartitionSpec as P

F32 = jnp.float32
BF16 = jnp.bfloat16
VMEM_ALL = 60 * 1024 * 1024


def spread_dense(row_panel, row_map, col_dense, row_count):
    targets = jnp.arange(row_count, dtype=jnp.int32)
    narrow = jnp.einsum("hik,hgk->hig", row_panel, col_dense, precision=lax.Precision.HIGHEST)
    row_hot = (row_map[:, :, None] == targets[None, None, :]).astype(jnp.float32)
    return jnp.einsum("hif,hig->fg", row_hot, narrow, precision=lax.Precision.HIGHEST)


def any_mesh(front_matrix, l_panels, l_map, u_panels, u_map):
    row_count, col_count = front_matrix.shape
    row_map = l_map[0, :, 0, :]
    col_map = u_map[0, :, 0, :]
    col_panel = lax.all_gather(u_panels, "row", axis=3, tiled=True)[0, :, 0]
    col_targets = jnp.arange(col_count, dtype=jnp.int32)
    col_hot = (col_map[:, :, None] == col_targets[None, None, :]).astype(jnp.float32)
    col_dense = jnp.einsum("hjg,hjk->hgk", col_hot, col_panel, precision=lax.Precision.HIGHEST)
    row_panel = lax.all_gather(l_panels, "col", axis=3, tiled=True)[0, :, 0]
    update = spread_dense(row_panel, row_map, col_dense, row_count)
    summed = lax.psum(update, "gz")
    return front_matrix - summed


def split(x):
    high = x.astype(BF16)
    return high, (x - high.astype(F32)).astype(BF16)


def dot(a, b):
    return jnp.dot(a, b, preferred_element_type=F32)


def dot_t(a, b):
    return lax.dot_general(a, b, (((1,), (1,)), ((), ())), preferred_element_type=F32)


def one_hot(slots, first, count):
    rows = lax.broadcasted_iota(jnp.int32, (count, slots.shape[-1]), 0) + first
    return jnp.where(rows == slots, 1.0, 0.0).astype(BF16)


def chunk_ids(here):
    low = here < 2
    return here, here ^ 1, jnp.where(low, 2, 1), jnp.where(low, 3, 0)


def dense_columns(slots, panel_ref, count):
    half = panel_ref.shape[0] // 2
    top = dot(one_hot(slots[:, :half], 0, count // 2), panel_ref[:half, :])
    return jnp.concatenate([top, dot(one_hot(slots, count // 2, count // 2), panel_ref[...])], axis=0)


def stage_kernel(plan, *refs):
    n_in, n_out = plan["inputs"], plan["outputs"]
    bases = [[refs[i] for i in pieces] for pieces in plan["bases"]]
    hbm_in, hbm_out = refs[:n_in], refs[n_in : n_in + n_out]
    scratch = refs[n_in + n_out :]
    held = dict(zip(plan["held"], scratch))
    acc, slots_ref, high_ref, low_ref = scratch[len(held) : len(held) + 4]
    n_staged = 2 * plan["emit"] + plan["sums"]
    staged = scratch[len(held) + 4 : len(held) + 4 + n_staged]
    extra = scratch[len(held) + 4 + n_staged : -4]
    panel_ref = scratch[-4]
    in_sem, base_sem, out_sem = scratch[-3:]
    ids = chunk_ids(lax.axis_index("col"))
    here = lax.axis_index("row")
    layer = lax.axis_index("gz")
    row_count, cols = acc.shape
    part, rows = plan["part"], plan["rows"]
    blocks = row_count // rows
    first_dense = n_out - n_staged

    def offset(first):
        return first(layer) if callable(first) else first

    def whole(i):
        lane = plan["held"].index(i)
        first, count = plan["range"][i]
        return pltpu.make_async_copy(hbm_in[i].at[pl.ds(first, count)], held[i], in_sem.at[lane, 0])

    def one(i, child):
        lane = plan["held"].index(i)
        first, _ = plan["range"][i]
        return pltpu.make_async_copy(hbm_in[i].at[first + child], held[i].at[child], in_sem.at[lane, child])

    def base_copy(n, block, piece=0, at_piece=0):
        at = pl.ds(pl.multiple_of(block * rows, rows), rows)
        target = acc if n == 0 else extra[n - 1]
        source = bases[n][piece].at[pl.ds(at_piece * rows, rows)]
        return pltpu.make_async_copy(source, target.at[at], base_sem.at[n, block])

    def dense_copy(n, child):
        return pltpu.make_async_copy(
            staged[n].at[child], hbm_out[first_dense + n].at[child], out_sem.at[1 + n, child]
        )

    each = blocks // plan["pieces"]

    def out_copy(block, piece):
        at = pl.ds(pl.multiple_of(block * rows, rows), rows)
        to = pl.ds(pl.multiple_of((block - piece * each) * rows, rows), rows)
        return pltpu.make_async_copy(acc.at[at], hbm_out[piece].at[to], out_sem.at[0, block])

    for i in plan["held"]:
        if i not in plan["single"]:
            whole(i).start()
    for group in plan["groups"]:
        for child in range(group["count"]):
            for i in group["dense"]:
                one(i, child).start()
    for block in range(blocks):
        for n, pieces in enumerate(bases):
            per = blocks // len(pieces)
            base_copy(n, block, block // per, block % per).start()
    for i in plan["held"]:
        if i not in plan["single"]:
            whole(i).wait()

    for group in plan["groups"]:

        def narrow(child, carry, group=group):
            if "u" in group:
                panels = [held[i][child] for i in group["u"][:3]]
                far_a, far_b = (held[i] for i in group["u"][3:])
                cut = group["cut"]
                in_a = far_a[jnp.minimum(child, cut - 1)]
                in_b = far_b[jnp.maximum(child - cut, 0)]
                panels.append(jnp.where(child < cut, in_a, in_b))
                for number, x in enumerate(panels):
                    high, low = split(x)
                    at = pl.ds(pl.multiple_of((here ^ number) * part, part), part)
                    panel_ref[at, :] = jnp.concatenate([high, low], axis=1)
                full = dense_columns(held[group["col_map"]][child], panel_ref, cols)
                depth = full.shape[1] // 2
                full_high, full_low = full[:, :depth], full[:, depth:]
                dense_high, dense_low = full_high.astype(BF16), full_low.astype(BF16)
                staged[0][child] = dense_high
                staged[1][child] = dense_low
                for n in range(2):
                    dense_copy(n, child).start()

                for c in range(plan["sums"]):

                    @pl.when(child == c)
                    def _(c=c):
                        staged[2 + c][0] = full_high + full_low
                        dense_copy(2 + c, 0).start()

            else:
                for i in group["dense"]:
                    one(i, child).wait()
                if len(group["dense"]) == 2:
                    dense_high, dense_low = (held[i][child] for i in group["dense"])
                else:
                    dense_high, dense_low = split(held[group["dense"][0]][child])
            panels = []
            for place, first, which, members in group["chunks"]:
                panels.append(sum(held[m][child] for m in members))
                at = pl.ds(pl.multiple_of((child + offset(first)) * part, part), part)
                slots_ref[place, :, at] = held[group["map"]][child, pl.ds(ids[which], 1), :]
            high, low = split(jnp.concatenate(panels, axis=0))
            both = dot_t(jnp.concatenate([high, low], axis=0), dense_high)
            count = high.shape[0]
            n_high, n_low = split(both[:count] + both[count:] + dot_t(high, dense_low))
            for number, (place, first, _, _) in enumerate(group["chunks"]):
                cut = slice(number * part, (number + 1) * part)
                at = pl.ds(pl.multiple_of((child + offset(first)) * part, part), part)
                high_ref[place, at, :] = n_high[cut]
                low_ref[place, at, :] = n_low[cut]
            return carry

        lax.fori_loop(0, group["count"], narrow, 0)

    spans = []
    for place, (_, count) in enumerate(plan["places"]):
        slots = slots_ref[place, :, : count * part].astype(F32)
        last = jnp.max(jnp.where(slots < row_count, slots, -1.0))
        spans.append((jnp.min(slots).astype(jnp.int32), last.astype(jnp.int32)))

    def finish(block, carry):
        at = pl.ds(pl.multiple_of(block * rows, rows), rows)
        if bases:
            for n in range(len(bases)):
                base_copy(n, block).wait()
            if plan["one_layer"]:

                @pl.when(layer != 0)
                def _():
                    acc[at, :] = jnp.zeros((rows, cols), F32)

            if len(bases) > 1:
                acc[at, :] += sum(e[at, :] for e in extra)
        else:
            acc[at, :] = jnp.zeros((rows, cols), F32)
        for place, (_, count) in enumerate(plan["places"]):
            used = count * part

            low, high = spans[place]

            @pl.when((low < (block + 1) * rows) & (high >= block * rows))
            def _(place=place, used=used):
                hot = one_hot(slots_ref[place, :, :used], block * rows, rows)
                acc[at, :] -= dot(hot, high_ref[place, :used]) + dot(hot, low_ref[place, :used])

        for piece in range(plan["pieces"]):

            @pl.when((block >= piece * each) & (block < (piece + 1) * each))
            def _(piece=piece):
                out_copy(block, piece).start()

        return carry

    lax.fori_loop(0, blocks, finish, 0)
    for block in range(blocks):
        out_copy(block, block // each).wait()
    for n in range(n_staged):
        for child in range(plan["groups"][0]["count"] if n < 2 else 1):
            dense_copy(n, child).wait()


def stage(shape, bases, places, groups, emit_sums=None, pieces=1, one_layer=False):
    row_count, col_count = shape
    inputs, base_at = [], []
    for base in bases:
        base_at.append(list(range(len(inputs), len(inputs) + len(base))))
        inputs += base
    held, ranges, single, layout = [], {}, [], []

    def take(pair, count):
        array, first = pair
        low, high = max(first, 0), min(first + count, array.shape[0])
        if high <= low:
            low, high = 0, 1
        inputs.append(array)
        held.append(len(inputs) - 1)
        ranges[held[-1]] = (low, high - low)
        return held[-1]

    for g in groups:
        count = g["count"]
        item = dict(count=count, map=take(g["map"], count), dense=[])
        if "u" in g:
            item["col_map"] = take(g["col_map"], count)
            item["u"] = [take(p, count) for p in g["u"]]
            item["cut"] = g["cut"]
        else:
            item["dense"] = [take(p, count) for p in g["dense"]]
            single += item["dense"]
        item["chunks"] = [
            (place, first, places[place][0], [take(p, count) for p in panels])
            for place, first, panels in g["chunks"]
        ]
        part, depth = g["chunks"][0][2][0][0].shape[1:]
        layout.append(item)
    rows = 2 * part
    most = max(count for _, count in places)
    total = groups[0]["count"]
    out_shape = [jax.ShapeDtypeStruct((row_count // pieces, col_count), F32)] * pieces
    emit = emit_sums is not None
    sums = emit_sums or 0
    dense_shapes = [((total, col_count, depth), BF16)] * (2 * emit) + [((1, col_count, depth), F32)] * sums
    out_shape += [jax.ShapeDtypeStruct(*x) for x in dense_shapes]
    plan = dict(
        inputs=len(inputs),
        outputs=len(out_shape),
        bases=base_at,
        pieces=pieces,
        held=held,
        range=ranges,
        single=single,
        groups=layout,
        places=places,
        emit=emit,
        sums=sums,
        one_layer=one_layer,
        part=part,
        rows=rows,
    )
    deepest = max(g["count"] for g in groups)
    blocks = row_count // rows
    kept = set(single)
    buffers = (
        [((ranges[i][1],) + inputs[i].shape[1:], inputs[i].dtype) for i in held]
        + [
            (shape, F32),
            ((len(places), 1, most * part), jnp.int32),
            ((len(places), most * part, col_count), BF16),
            ((len(places), most * part, col_count), BF16),
        ]
        + dense_shapes
        + [(shape, F32)] * max(len(bases) - 1, 0)
        + [((4 * part, 2 * depth), BF16)]
    )
    return pl.pallas_call(
        functools.partial(stage_kernel, plan),
        in_specs=[pl.BlockSpec(memory_space=pl.ANY if i in kept else pltpu.HBM) for i in range(len(inputs))],
        out_specs=[pl.BlockSpec(memory_space=pltpu.HBM)] * pieces + [pl.BlockSpec(memory_space=pl.ANY)] * len(dense_shapes),
        out_shape=out_shape,
        scratch_shapes=[pltpu.VMEM(dims, kind) for dims, kind in buffers]
        + [
            pltpu.SemaphoreType.DMA((len(held), deepest)),
            pltpu.SemaphoreType.DMA((max(len(bases), 1), blocks)),
            pltpu.SemaphoreType.DMA((1 + len(dense_shapes), max(blocks, total))),
        ],
        compiler_params=pltpu.CompilerParams(vmem_limit_bytes=VMEM_ALL),
        cost_estimate=pl.CostEstimate(flops=1000, bytes_accessed=1000, transcendentals=0),
    )(*inputs)


ENDS = [(0, 1), (1, 0), (2, 3), (3, 2)]
MIDDLE = [(1, 2), (2, 1)]
OUTWARD = [(1, 0), (2, 3)]
SWAP_X = [(0, 1), (1, 0), (2, 3), (3, 2)]
SWAP_Y = [(0, 2), (2, 0), (1, 3), (3, 1)]
SWAP_XY = [(0, 3), (3, 0), (1, 2), (2, 1)]


def four_by_four(front_matrix, l_panels, l_map, u_panels, u_map):
    shape = front_matrix.shape
    l_own = l_panels[0, :, 0]
    u_own = u_panels[0, :, 0]
    children = u_own.shape[0]
    first = children // 2
    late = children // 4
    rest, early = children - first, children - late
    row_map = l_map.reshape(children, 4, -1)
    col_map = u_map.reshape(children, 1, -1)
    swap = [(0, 1), (1, 0)]
    together = lax.optimization_barrier

    pair = lax.ppermute(l_own, "col", ENDS)
    mid_b = lax.ppermute(l_own, "col", MIDDLE)
    by_x = lax.ppermute(u_own, "row", SWAP_X)
    by_y = lax.ppermute(u_own, "row", SWAP_Y)
    pair, by_x, by_y = together((pair, by_x, by_y))

    def diagonal(start, count):
        cut = start + count // 2
        return (
            lax.ppermute(by_x[start:cut], "row", SWAP_Y),
            lax.ppermute(by_y[cut : start + count], "row", SWAP_X),
        )

    mid_a = lax.ppermute(mid_b, "col", OUTWARD)
    far_b = lax.ppermute(pair, "col", MIDDLE)
    by_xy1 = diagonal(0, first)
    by_xy2 = diagonal(first, rest)
    row_map_other = lax.ppermute(row_map, "gz", swap)

    def near(base, start, count, u, chunks=(), groups=(), **options):
        group = dict(
            count=count,
            map=(row_map, start),
            col_map=(col_map, start),
            u=[(u_own, start), (by_x, start), (by_y, start)] + [(x, 0) for x in u],
            cut=count // 2,
            chunks=[(0, 0, [(l_own, start)]), (1, 0, [(pair, start)]), *chunks],
        )
        places = [(0, count), (1, count)] + [(2, children)] * len(chunks)
        return stage(shape, [base], places, [group, *groups], **options)

    mine, *dense1 = near([front_matrix], 0, first, by_xy1, emit_sums=late, one_layer=True)
    dense1, sums = dense1[:2], dense1[2:]
    far_b, mid_a, mine = together((far_b, mid_a, mine))
    far_b2, far_b1 = far_b[:late], far_b[late:]
    far_a1 = lax.ppermute(far_b1, "col", OUTWARD)
    far_a2 = lax.ppermute(far_b2, "col", OUTWARD)
    far_b2_other = lax.ppermute(far_b2, "gz", swap)
    *sums, by_xy2a, by_xy2b = together((*sums, *by_xy2))
    sums_other = [lax.ppermute(x, "gz", swap) for x in sums]
    mine, *dense2 = near(
        [mine],
        first,
        rest,
        (by_xy2a, by_xy2b),
        [(2, first, [(mid_a, first), (mid_b, first)])],
        [
            dict(
                count=first,
                map=(row_map, 0),
                dense=[(d, 0) for d in dense1],
                chunks=[(2, 0, [(mid_a, 0), (mid_b, 0)])],
            )
        ],
        emit_sums=0,
    )
    mine, far_b2_other, *sums_other = together((mine, far_b2_other, *sums_other))
    top, bottom = stage(
        shape,
        [[mine]],
        [(3, early)],
        [
            dict(
                count=first - late,
                map=(row_map, late),
                dense=[(d, late) for d in dense1],
                chunks=[(0, 0, [(far_a1, 0), (far_b1, 0)])],
            ),
            dict(
                count=rest,
                map=(row_map, first),
                dense=[(d, 0) for d in dense2],
                chunks=[(0, first - late, [(far_a1, first - late), (far_b1, first - late)])],
            ),
        ],
        pieces=2,
    )
    other_top = lax.ppermute(top, "gz", swap)
    sent, far_a2 = together((bottom, far_a2))
    far_a2_other = lax.ppermute(far_a2, "gz", swap)
    other_bottom = lax.ppermute(sent, "gz", swap)
    late_groups = [
        dict(
            count=1,
            map=(slot_map, c),
            dense=[(x, 0)],
            chunks=[(0, at, [(far, c) for far in fars])],
        )
        for slot_map, denses, fars, at in (
            (row_map, sums, (far_a2, far_b2), lambda layer: layer * late),
            (row_map_other, sums_other, (far_a2_other, far_b2_other), lambda layer: (1 - layer) * late),
        )
        for c, x in enumerate(denses)
    ]
    for g in late_groups:
        place, at, fars = g["chunks"][0]
        g["chunks"] = [(place, functools.partial(lambda at, c, layer: at(layer) + c, at, g["map"][1]), fars)]
    (out,) = stage(shape, [[top, bottom], [other_top, other_bottom]], [(3, 2 * late)], late_groups)
    return out


def solution(mesh):
    placed = (
        P("row", "col"),
        P("gz", None, "row", "col", None),
        P("gz", None, "row", None),
        P("gz", None, "col", "row", None),
        P("gz", None, "col", None),
    )
    square = mesh.shape["row"] == 4 and mesh.shape["col"] == 4
    return jax.shard_map(
        four_by_four if square else any_mesh,
        mesh=mesh,
        in_specs=placed,
        out_specs=P("row", "col"),
        check_vma=False,
    )
```

```python
import functools

import jax
import jax.numpy as jnp
from jax import lax
from jax.experimental import pallas as pl
from jax.experimental.pallas import tpu as pltpu
from jax.sharding import PartitionSpec as P

F32 = jnp.float32
BF16 = jnp.bfloat16
VMEM_ALL = 60 * 1024 * 1024


def spread_dense(row_panel, row_map, col_dense, row_count):
    targets = jnp.arange(row_count, dtype=jnp.int32)
    narrow = jnp.einsum("hik,hgk->hig", row_panel, col_dense, precision=lax.Precision.HIGHEST)
    row_hot = (row_map[:, :, None] == targets[None, None, :]).astype(jnp.float32)
    return jnp.einsum("hif,hig->fg", row_hot, narrow, precision=lax.Precision.HIGHEST)


def any_mesh(front_matrix, l_panels, l_map, u_panels, u_map):
    row_count, col_count = front_matrix.shape
    row_map = l_map[0, :, 0, :]
    col_map = u_map[0, :, 0, :]
    col_panel = lax.all_gather(u_panels, "row", axis=3, tiled=True)[0, :, 0]
    col_targets = jnp.arange(col_count, dtype=jnp.int32)
    col_hot = (col_map[:, :, None] == col_targets[None, None, :]).astype(jnp.float32)
    col_dense = jnp.einsum("hjg,hjk->hgk", col_hot, col_panel, precision=lax.Precision.HIGHEST)
    row_panel = lax.all_gather(l_panels, "col", axis=3, tiled=True)[0, :, 0]
    update = spread_dense(row_panel, row_map, col_dense, row_count)
    summed = lax.psum(update, "gz")
    return front_matrix - summed


def split(x):
    high = x.astype(BF16)
    return high, (x - high.astype(F32)).astype(BF16)


def dot(a, b):
    return jnp.dot(a, b, preferred_element_type=F32)


def dot_t(a, b):
    return lax.dot_general(a, b, (((1,), (1,)), ((), ())), preferred_element_type=F32)


def one_hot(slots, first, count):
    rows = lax.broadcasted_iota(jnp.int32, (count, slots.shape[-1]), 0) + first
    return jnp.where(rows == slots, 1.0, 0.0).astype(BF16)


def chunk_ids(here):
    low = here < 2
    return here, here ^ 1, jnp.where(low, 2, 1), jnp.where(low, 3, 0)


def dense_columns(slots, panel_ref, count):
    half = panel_ref.shape[0] // 2
    top = dot(one_hot(slots[:, :half], 0, count // 2), panel_ref[:half, :])
    return jnp.concatenate([top, dot(one_hot(slots, count // 2, count // 2), panel_ref[...])], axis=0)


def stage_kernel(plan, *refs):
    n_in, n_out = plan["inputs"], plan["outputs"]
    bases = [[refs[i] for i in pieces] for pieces in plan["bases"]]
    hbm_in, hbm_out = refs[:n_in], refs[n_in : n_in + n_out]
    scratch = refs[n_in + n_out :]
    held = dict(zip(plan["held"], scratch))
    acc, slots_ref, high_ref, low_ref = scratch[len(held) : len(held) + 4]
    n_staged = 2 * plan["emit"] + plan["sums"]
    staged = scratch[len(held) + 4 : len(held) + 4 + n_staged]
    extra = scratch[len(held) + 4 + n_staged : -4]
    panel_ref = scratch[-4]
    in_sem, base_sem, out_sem = scratch[-3:]
    ids = chunk_ids(lax.axis_index("col"))
    here = lax.axis_index("row")
    layer = lax.axis_index("gz")
    row_count, cols = acc.shape
    part, rows = plan["part"], plan["rows"]
    blocks = row_count // rows
    first_dense = n_out - n_staged

    def offset(first):
        return first(layer) if callable(first) else first

    def whole(i):
        lane = plan["held"].index(i)
        first, count = plan["range"][i]
        return pltpu.make_async_copy(hbm_in[i].at[pl.ds(first, count)], held[i], in_sem.at[lane, 0])

    def one(i, child):
        lane = plan["held"].index(i)
        first, _ = plan["range"][i]
        return pltpu.make_async_copy(hbm_in[i].at[first + child], held[i].at[child], in_sem.at[lane, child])

    def base_copy(n, block, piece=0, at_piece=0):
        at = pl.ds(pl.multiple_of(block * rows, rows), rows)
        target = acc if n == 0 else extra[n - 1]
        source = bases[n][piece].at[pl.ds(at_piece * rows, rows)]
        return pltpu.make_async_copy(source, target.at[at], base_sem.at[n, block])

    def dense_copy(n, child):
        return pltpu.make_async_copy(
            staged[n].at[child], hbm_out[first_dense + n].at[child], out_sem.at[1 + n, child]
        )

    each = blocks // plan["pieces"]

    def out_copy(block, piece):
        at = pl.ds(pl.multiple_of(block * rows, rows), rows)
        to = pl.ds(pl.multiple_of((block - piece * each) * rows, rows), rows)
        return pltpu.make_async_copy(acc.at[at], hbm_out[piece].at[to], out_sem.at[0, block])

    for i in plan["held"]:
        if i not in plan["single"]:
            whole(i).start()
    for group in plan["groups"]:
        for child in range(group["count"]):
            for i in group["each"]:
                one(i, child).start()
    for block in range(blocks):
        for n, pieces in enumerate(bases):
            per = blocks // len(pieces)
            base_copy(n, block, block // per, block % per).start()
    for i in plan["held"]:
        if i not in plan["single"]:
            whole(i).wait()

    for group in plan["groups"]:

        def narrow(child, carry, group=group):
            for i in group["each"]:
                one(i, child).wait()
            if "u" in group:
                panels = [held[i][child] for i in group["u"][:3]]
                far_a, far_b = (held[i] for i in group["u"][3:])
                cut = group["cut"]
                in_a = far_a[jnp.minimum(child, cut - 1)]
                in_b = far_b[jnp.maximum(child - cut, 0)]
                panels.append(jnp.where(child < cut, in_a, in_b))
                for number, x in enumerate(panels):
                    high, low = split(x)
                    at = pl.ds(pl.multiple_of((here ^ number) * part, part), part)
                    panel_ref[at, :] = jnp.concatenate([high, low], axis=1)
                full = dense_columns(held[group["col_map"]][child], panel_ref, cols)
                depth = full.shape[1] // 2
                full_high, full_low = full[:, :depth], full[:, depth:]
                dense_high, dense_low = full_high.astype(BF16), full_low.astype(BF16)
                staged[0][child] = dense_high
                staged[1][child] = dense_low
                for n in range(2):
                    dense_copy(n, child).start()

                for c in range(plan["sums"]):

                    @pl.when(child == c)
                    def _(c=c):
                        staged[2 + c][0] = full_high + full_low
                        dense_copy(2 + c, 0).start()

            elif len(group["dense"]) == 2:
                dense_high, dense_low = (held[i][child] for i in group["dense"])
            else:
                dense_high, dense_low = split(held[group["dense"][0]][child])
            panels = []
            for place, first, which, members in group["chunks"]:
                panels.append(sum(held[m][child] for m in members))
                at = pl.ds(pl.multiple_of((child + offset(first)) * part, part), part)
                slots_ref[place, :, at] = held[group["map"]][child, pl.ds(ids[which], 1), :]
            high, low = split(jnp.concatenate(panels, axis=0))
            both = dot_t(jnp.concatenate([high, low], axis=0), dense_high)
            count = high.shape[0]
            n_high, n_low = split(both[:count] + both[count:] + dot_t(high, dense_low))
            for number, (place, first, _, _) in enumerate(group["chunks"]):
                cut = slice(number * part, (number + 1) * part)
                at = pl.ds(pl.multiple_of((child + offset(first)) * part, part), part)
                high_ref[place, at, :] = n_high[cut]
                low_ref[place, at, :] = n_low[cut]
            return carry

        lax.fori_loop(0, group["count"], narrow, 0)

    spans = []
    for place, (_, count) in enumerate(plan["places"]):
        slots = slots_ref[place, :, : count * part].astype(F32)
        last = jnp.max(jnp.where(slots < row_count, slots, -1.0))
        spans.append((jnp.min(slots).astype(jnp.int32), last.astype(jnp.int32)))

    def finish(block, carry):
        at = pl.ds(pl.multiple_of(block * rows, rows), rows)
        if bases:
            for n in range(len(bases)):
                base_copy(n, block).wait()
            if plan["one_layer"]:

                @pl.when(layer != 0)
                def _():
                    acc[at, :] = jnp.zeros((rows, cols), F32)

            if len(bases) > 1:
                acc[at, :] += sum(e[at, :] for e in extra)
        else:
            acc[at, :] = jnp.zeros((rows, cols), F32)
        for place, (_, count) in enumerate(plan["places"]):
            used = count * part

            low, high = spans[place]

            @pl.when((low < (block + 1) * rows) & (high >= block * rows))
            def _(place=place, used=used):
                hot = one_hot(slots_ref[place, :, :used], block * rows, rows)
                acc[at, :] -= dot(hot, high_ref[place, :used]) + dot(hot, low_ref[place, :used])

        for piece in range(plan["pieces"]):

            @pl.when((block >= piece * each) & (block < (piece + 1) * each))
            def _(piece=piece):
                out_copy(block, piece).start()

        return carry

    lax.fori_loop(0, blocks, finish, 0)
    for block in range(blocks):
        out_copy(block, block // each).wait()
    for n in range(n_staged):
        for child in range(plan["groups"][0]["count"] if n < 2 else 1):
            dense_copy(n, child).wait()


def stage(shape, bases, places, groups, emit_sums=None, pieces=1, one_layer=False):
    row_count, col_count = shape
    inputs, base_at = [], []
    for base in bases:
        base_at.append(list(range(len(inputs), len(inputs) + len(base))))
        inputs += base
    held, ranges, single, kept, layout = [], {}, [], [], []

    def take(pair, count):
        array, first = pair
        low, high = max(first, 0), min(first + count, array.shape[0])
        if high <= low:
            low, high = 0, 1
        inputs.append(array)
        held.append(len(inputs) - 1)
        ranges[held[-1]] = (low, high - low)
        return held[-1]

    for g in groups:
        count = g["count"]
        item = dict(count=count, map=take(g["map"], count), dense=[])
        if "u" in g:
            item["col_map"] = take(g["col_map"], count)
            item["u"] = [take(p, count) for p in g["u"]]
            item["each"] = item["u"][:3]
            item["cut"] = g["cut"]
        else:
            item["dense"] = [take(p, count) for p in g["dense"]]
            kept += item["dense"]
            item["each"] = list(item["dense"])
        item["chunks"] = [
            (place, first, places[place][0], [take(p, count) for p in panels])
            for place, first, panels in g["chunks"]
        ]
        for _, _, _, members in item["chunks"]:
            item["each"] += members
        single += item["each"]
        part, depth = g["chunks"][0][2][0][0].shape[1:]
        layout.append(item)
    rows = 2 * part
    most = max(count for _, count in places)
    total = groups[0]["count"]
    out_shape = [jax.ShapeDtypeStruct((row_count // pieces, col_count), F32)] * pieces
    emit = emit_sums is not None
    sums = emit_sums or 0
    dense_shapes = [((total, col_count, depth), BF16)] * (2 * emit) + [((1, col_count, depth), F32)] * sums
    out_shape += [jax.ShapeDtypeStruct(*x) for x in dense_shapes]
    plan = dict(
        inputs=len(inputs),
        outputs=len(out_shape),
        bases=base_at,
        pieces=pieces,
        held=held,
        range=ranges,
        single=single,
        groups=layout,
        places=places,
        emit=emit,
        sums=sums,
        one_layer=one_layer,
        part=part,
        rows=rows,
    )
    deepest = max(g["count"] for g in groups)
    blocks = row_count // rows
    buffers = (
        [((ranges[i][1],) + inputs[i].shape[1:], inputs[i].dtype) for i in held]
        + [
            (shape, F32),
            ((len(places), 1, most * part), jnp.int32),
            ((len(places), most * part, col_count), BF16),
            ((len(places), most * part, col_count), BF16),
        ]
        + dense_shapes
        + [(shape, F32)] * max(len(bases) - 1, 0)
        + [((4 * part, 2 * depth), BF16)]
    )
    return pl.pallas_call(
        functools.partial(stage_kernel, plan),
        in_specs=[pl.BlockSpec(memory_space=pl.ANY if i in kept else pltpu.HBM) for i in range(len(inputs))],
        out_specs=[pl.BlockSpec(memory_space=pltpu.HBM)] * pieces + [pl.BlockSpec(memory_space=pl.ANY)] * len(dense_shapes),
        out_shape=out_shape,
        scratch_shapes=[pltpu.VMEM(dims, kind) for dims, kind in buffers]
        + [
            pltpu.SemaphoreType.DMA((len(held), deepest)),
            pltpu.SemaphoreType.DMA((max(len(bases), 1), blocks)),
            pltpu.SemaphoreType.DMA((1 + len(dense_shapes), max(blocks, total))),
        ],
        compiler_params=pltpu.CompilerParams(vmem_limit_bytes=VMEM_ALL),
        cost_estimate=pl.CostEstimate(flops=1000, bytes_accessed=1000, transcendentals=0),
    )(*inputs)


ENDS = [(0, 1), (1, 0), (2, 3), (3, 2)]
MIDDLE = [(1, 2), (2, 1)]
OUTWARD = [(1, 0), (2, 3)]
SWAP_X = [(0, 1), (1, 0), (2, 3), (3, 2)]
SWAP_Y = [(0, 2), (2, 0), (1, 3), (3, 1)]
SWAP_XY = [(0, 3), (3, 0), (1, 2), (2, 1)]


def four_by_four(front_matrix, l_panels, l_map, u_panels, u_map):
    shape = front_matrix.shape
    l_own = l_panels[0, :, 0]
    u_own = u_panels[0, :, 0]
    children = u_own.shape[0]
    first = children // 2
    late = children // 4
    rest, early = children - first, children - late
    row_map = l_map.reshape(children, 4, -1)
    col_map = u_map.reshape(children, 1, -1)
    swap = [(0, 1), (1, 0)]
    together = lax.optimization_barrier

    pair = lax.ppermute(l_own, "col", ENDS)
    mid_b = lax.ppermute(l_own, "col", MIDDLE)
    by_x = lax.ppermute(u_own, "row", SWAP_X)
    by_y = lax.ppermute(u_own, "row", SWAP_Y)
    pair, by_x, by_y = together((pair, by_x, by_y))

    def diagonal(start, count):
        cut = start + count // 2
        return (
            lax.ppermute(by_x[start:cut], "row", SWAP_Y),
            lax.ppermute(by_y[cut : start + count], "row", SWAP_X),
        )

    mid_a = lax.ppermute(mid_b, "col", OUTWARD)
    far_b = lax.ppermute(pair, "col", MIDDLE)
    by_xy1 = diagonal(0, first)
    by_xy2 = diagonal(first, rest)
    row_map_other = lax.ppermute(row_map, "gz", swap)

    def near(base, start, count, u, chunks=(), groups=(), **options):
        group = dict(
            count=count,
            map=(row_map, start),
            col_map=(col_map, start),
            u=[(u_own, start), (by_x, start), (by_y, start)] + [(x, 0) for x in u],
            cut=count // 2,
            chunks=[(0, 0, [(l_own, start)]), (1, 0, [(pair, start)]), *chunks],
        )
        places = [(0, count), (1, count)] + [(2, children)] * len(chunks)
        return stage(shape, [base], places, [group, *groups], **options)

    mine, *dense1 = near([front_matrix], 0, first, by_xy1, emit_sums=late, one_layer=True)
    dense1, sums = dense1[:2], dense1[2:]
    far_b, mid_a, mine = together((far_b, mid_a, mine))
    far_b2, far_b1 = far_b[:late], far_b[late:]
    far_a1 = lax.ppermute(far_b1, "col", OUTWARD)
    far_a2 = lax.ppermute(far_b2, "col", OUTWARD)
    far_b2_other = lax.ppermute(far_b2, "gz", swap)
    *sums, by_xy2a, by_xy2b = together((*sums, *by_xy2))
    sums_other = [lax.ppermute(x, "gz", swap) for x in sums]
    mine, *dense2 = near(
        [mine],
        first,
        rest,
        (by_xy2a, by_xy2b),
        [(2, first, [(mid_a, first), (mid_b, first)])],
        [
            dict(
                count=first,
                map=(row_map, 0),
                dense=[(d, 0) for d in dense1],
                chunks=[(2, 0, [(mid_a, 0), (mid_b, 0)])],
            )
        ],
        emit_sums=0,
    )
    mine, far_b2_other, *sums_other = together((mine, far_b2_other, *sums_other))
    top, bottom = stage(
        shape,
        [[mine]],
        [(3, early)],
        [
            dict(
                count=first - late,
                map=(row_map, late),
                dense=[(d, late) for d in dense1],
                chunks=[(0, 0, [(far_a1, 0), (far_b1, 0)])],
            ),
            dict(
                count=rest,
                map=(row_map, first),
                dense=[(d, 0) for d in dense2],
                chunks=[(0, first - late, [(far_a1, first - late), (far_b1, first - late)])],
            ),
        ],
        pieces=2,
    )
    other_top = lax.ppermute(top, "gz", swap)
    sent, far_a2 = together((bottom, far_a2))
    far_a2_other = lax.ppermute(far_a2, "gz", swap)
    other_bottom = lax.ppermute(sent, "gz", swap)
    late_groups = [
        dict(
            count=1,
            map=(slot_map, c),
            dense=[(x, 0)],
            chunks=[(0, at, [(far, c) for far in fars])],
        )
        for slot_map, denses, fars, at in (
            (row_map, sums, (far_a2, far_b2), lambda layer: layer * late),
            (row_map_other, sums_other, (far_a2_other, far_b2_other), lambda layer: (1 - layer) * late),
        )
        for c, x in enumerate(denses)
    ]
    for g in late_groups:
        place, at, fars = g["chunks"][0]
        g["chunks"] = [(place, functools.partial(lambda at, c, layer: at(layer) + c, at, g["map"][1]), fars)]
    (out,) = stage(shape, [[top, bottom], [other_top, other_bottom]], [(3, 2 * late)], late_groups)
    return out


def solution(mesh):
    placed = (
        P("row", "col"),
        P("gz", None, "row", "col", None),
        P("gz", None, "row", None),
        P("gz", None, "col", "row", None),
        P("gz", None, "col", None),
    )
    square = mesh.shape["row"] == 4 and mesh.shape["col"] == 4
    return jax.shard_map(
        four_by_four if square else any_mesh,
        mesh=mesh,
        in_specs=placed,
        out_specs=P("row", "col"),
        check_vma=False,
    )
```

```python
import functools

import jax
import jax.numpy as jnp
from jax import lax
from jax.experimental import pallas as pl
from jax.experimental.pallas import tpu as pltpu
from jax.sharding import PartitionSpec as P

F32 = jnp.float32
BF16 = jnp.bfloat16
VMEM_ALL = 127 * 512 * 1024


def spread_dense(row_panel, row_map, col_dense, row_count):
    targets = jnp.arange(row_count, dtype=jnp.int32)
    narrow = jnp.einsum("hik,hgk->hig", row_panel, col_dense, precision=lax.Precision.HIGHEST)
    row_hot = (row_map[:, :, None] == targets[None, None, :]).astype(jnp.float32)
    return jnp.einsum("hif,hig->fg", row_hot, narrow, precision=lax.Precision.HIGHEST)


def any_mesh(front_matrix, l_panels, l_map, u_panels, u_map):
    row_count, col_count = front_matrix.shape
    row_map = l_map[0, :, 0, :]
    col_map = u_map[0, :, 0, :]
    col_panel = lax.all_gather(u_panels, "row", axis=3, tiled=True)[0, :, 0]
    col_targets = jnp.arange(col_count, dtype=jnp.int32)
    col_hot = (col_map[:, :, None] == col_targets[None, None, :]).astype(jnp.float32)
    col_dense = jnp.einsum("hjg,hjk->hgk", col_hot, col_panel, precision=lax.Precision.HIGHEST)
    row_panel = lax.all_gather(l_panels, "col", axis=3, tiled=True)[0, :, 0]
    update = spread_dense(row_panel, row_map, col_dense, row_count)
    summed = lax.psum(update, "gz")
    return front_matrix - summed


def split(x):
    high = x.astype(BF16)
    return high, (x - high.astype(F32)).astype(BF16)


def dot(a, b):
    return jnp.dot(a, b, preferred_element_type=F32)


def dot_t(a, b):
    return lax.dot_general(a, b, (((1,), (1,)), ((), ())), preferred_element_type=F32)


def one_hot(slots, first, count):
    rows = lax.broadcasted_iota(jnp.int32, (count, slots.shape[-1]), 0) + first
    return jnp.where(rows == slots, 1.0, 0.0).astype(BF16)


def chunk_ids(here):
    low = here < 2
    return here, here ^ 1, jnp.where(low, 2, 1), jnp.where(low, 3, 0)


def dense_columns(slots, panel_ref, count):
    half = panel_ref.shape[0] // 2
    top = dot(one_hot(slots[:, :half], 0, count // 2), panel_ref[:half, :])
    return jnp.concatenate([top, dot(one_hot(slots, count // 2, count // 2), panel_ref[...])], axis=0)


def stage_kernel(plan, *refs):
    n_in, n_out = plan["inputs"], plan["outputs"]
    bases = [[refs[i] for i in pieces] for pieces in plan["bases"]]
    hbm_in, hbm_out = refs[:n_in], refs[n_in : n_in + n_out]
    scratch = refs[n_in + n_out :]
    held = dict(zip(plan["held"], scratch))
    acc, slots_ref, high_ref, low_ref = scratch[len(held) : len(held) + 4]
    n_staged = 2 * plan["emit"] + plan["sums"]
    staged = scratch[len(held) + 4 : len(held) + 4 + n_staged]
    extra = scratch[len(held) + 4 + n_staged : -4]
    panel_ref = scratch[-4]
    in_sem, base_sem, out_sem = scratch[-3:]
    ids = chunk_ids(lax.axis_index("col"))
    here = lax.axis_index("row")
    layer = lax.axis_index("gz")
    row_count, cols = acc.shape
    part, rows = plan["part"], plan["rows"]
    blocks = row_count // rows
    first_dense = n_out - n_staged

    def offset(first):
        return first(layer) if callable(first) else first

    def whole(i):
        lane = plan["held"].index(i)
        first, count = plan["range"][i]
        return pltpu.make_async_copy(hbm_in[i].at[pl.ds(first, count)], held[i], in_sem.at[lane, 0])

    def one(i, child):
        lane = plan["held"].index(i)
        first, _ = plan["range"][i]
        return pltpu.make_async_copy(hbm_in[i].at[first + child], held[i].at[child], in_sem.at[lane, child])

    def base_copy(n, block, piece=0, at_piece=0):
        at = pl.ds(pl.multiple_of(block * rows, rows), rows)
        target = acc if n == 0 else extra[n - 1]
        source = bases[n][piece].at[pl.ds(at_piece * rows, rows)]
        return pltpu.make_async_copy(source, target.at[at], base_sem.at[n, block])

    def dense_copy(n, child):
        return pltpu.make_async_copy(
            staged[n].at[child], hbm_out[first_dense + n].at[child], out_sem.at[1 + n, child]
        )

    each = blocks // plan["pieces"]

    def out_copy(block, piece):
        at = pl.ds(pl.multiple_of(block * rows, rows), rows)
        to = pl.ds(pl.multiple_of((block - piece * each) * rows, rows), rows)
        return pltpu.make_async_copy(acc.at[at], hbm_out[piece].at[to], out_sem.at[0, block])

    for i in plan["held"]:
        if i not in plan["single"]:
            whole(i).start()
    for group in plan["groups"]:
        for child in range(group["count"]):
            for i in group["each"]:
                one(i, child).start()
    for block in range(blocks):
        for n, pieces in enumerate(bases):
            per = blocks // len(pieces)
            base_copy(n, block, block // per, block % per).start()
    for i in plan["held"]:
        if i not in plan["single"]:
            whole(i).wait()

    for group in plan["groups"]:

        def narrow(child, carry, group=group):
            for i in group["each"]:
                one(i, child).wait()
            if "u" in group:
                panels = [held[i][child] for i in group["u"][:3]]
                far_a, far_b = (held[i] for i in group["u"][3:])
                cut = group["cut"]
                in_a = far_a[jnp.minimum(child, cut - 1)]
                in_b = far_b[jnp.maximum(child - cut, 0)]
                panels.append(jnp.where(child < cut, in_a, in_b))
                for number, x in enumerate(panels):
                    high, low = split(x)
                    at = pl.ds(pl.multiple_of((here ^ number) * part, part), part)
                    panel_ref[at, :] = jnp.concatenate([high, low], axis=1)
                full = dense_columns(held[group["col_map"]][child], panel_ref, cols)
                depth = full.shape[1] // 2
                full_high, full_low = full[:, :depth], full[:, depth:]
                dense_high, dense_low = full_high.astype(BF16), full_low.astype(BF16)
                staged[0][child] = dense_high
                staged[1][child] = dense_low
                for n in range(2):
                    dense_copy(n, child).start()

                for c in range(plan["sums"]):

                    @pl.when(child == c)
                    def _(c=c):
                        staged[2 + c][0] = full_high + full_low
                        dense_copy(2 + c, 0).start()

            elif len(group["dense"]) == 2:
                dense_high, dense_low = (held[i][child] for i in group["dense"])
            else:
                dense_high, dense_low = split(held[group["dense"][0]][child])
            panels = []
            for place, first, which, members in group["chunks"]:
                panels.append(sum(held[m][child] for m in members))
                at = pl.ds(pl.multiple_of((child + offset(first)) * part, part), part)
                slots_ref[place, :, at] = held[group["map"]][child, pl.ds(ids[which], 1), :]
            high, low = split(jnp.concatenate(panels, axis=0))
            both = dot_t(jnp.concatenate([high, low], axis=0), dense_high)
            count = high.shape[0]
            n_high, n_low = split(both[:count] + both[count:] + dot_t(high, dense_low))
            for number, (place, first, _, _) in enumerate(group["chunks"]):
                cut = slice(number * part, (number + 1) * part)
                at = pl.ds(pl.multiple_of((child + offset(first)) * part, part), part)
                high_ref[place, at, :] = n_high[cut]
                low_ref[place, at, :] = n_low[cut]
            return carry

        lax.fori_loop(0, group["count"], narrow, 0)

    spans = []
    for place, (_, count) in enumerate(plan["places"]):
        slots = slots_ref[place, :, : count * part].astype(F32)
        last = jnp.max(jnp.where(slots < row_count, slots, -1.0))
        spans.append((jnp.min(slots).astype(jnp.int32), last.astype(jnp.int32)))

    def finish(block, carry):
        at = pl.ds(pl.multiple_of(block * rows, rows), rows)
        if bases:
            for n in range(len(bases)):
                base_copy(n, block).wait()
            if plan["one_layer"]:

                @pl.when(layer != 0)
                def _():
                    acc[at, :] = jnp.zeros((rows, cols), F32)

            if len(bases) > 1:
                acc[at, :] += sum(e[at, :] for e in extra)
        else:
            acc[at, :] = jnp.zeros((rows, cols), F32)
        for place, (_, count) in enumerate(plan["places"]):
            used = count * part

            low, high = spans[place]

            @pl.when((low < (block + 1) * rows) & (high >= block * rows))
            def _(place=place, used=used):
                hot = one_hot(slots_ref[place, :, :used], block * rows, rows)
                acc[at, :] -= dot(hot, high_ref[place, :used]) + dot(hot, low_ref[place, :used])

        for piece in range(plan["pieces"]):

            @pl.when((block >= piece * each) & (block < (piece + 1) * each))
            def _(piece=piece):
                out_copy(block, piece).start()

        return carry

    lax.fori_loop(0, blocks, finish, 0)
    for block in range(blocks):
        out_copy(block, block // each).wait()
    for n in range(n_staged):
        for child in range(plan["groups"][0]["count"] if n < 2 else 1):
            dense_copy(n, child).wait()


def stage(shape, bases, places, groups, emit_sums=None, pieces=1, one_layer=False):
    row_count, col_count = shape
    inputs, base_at = [], []
    for base in bases:
        base_at.append(list(range(len(inputs), len(inputs) + len(base))))
        inputs += base
    held, ranges, single, kept, layout = [], {}, [], [], []

    def take(pair, count):
        array, first = pair
        low, high = max(first, 0), min(first + count, array.shape[0])
        if high <= low:
            low, high = 0, 1
        inputs.append(array)
        held.append(len(inputs) - 1)
        ranges[held[-1]] = (low, high - low)
        return held[-1]

    for g in groups:
        count = g["count"]
        item = dict(count=count, map=take(g["map"], count), dense=[])
        if "u" in g:
            item["col_map"] = take(g["col_map"], count)
            item["u"] = [take(p, count) for p in g["u"]]
            item["each"] = item["u"][:3]
            item["cut"] = g["cut"]
        else:
            item["dense"] = [take(p, count) for p in g["dense"]]
            kept += item["dense"]
            item["each"] = list(item["dense"])
        item["chunks"] = [
            (place, first, places[place][0], [take(p, count) for p in panels])
            for place, first, panels in g["chunks"]
        ]
        for _, _, _, members in item["chunks"]:
            item["each"] += members
        single += item["each"]
        part, depth = g["chunks"][0][2][0][0].shape[1:]
        layout.append(item)
    rows = 2 * part
    most = max(count for _, count in places)
    total = groups[0]["count"]
    out_shape = [jax.ShapeDtypeStruct((row_count // pieces, col_count), F32)] * pieces
    emit = emit_sums is not None
    sums = emit_sums or 0
    dense_shapes = [((total, col_count, depth), BF16)] * (2 * emit) + [((1, col_count, depth), F32)] * sums
    out_shape += [jax.ShapeDtypeStruct(*x) for x in dense_shapes]
    plan = dict(
        inputs=len(inputs),
        outputs=len(out_shape),
        bases=base_at,
        pieces=pieces,
        held=held,
        range=ranges,
        single=single,
        groups=layout,
        places=places,
        emit=emit,
        sums=sums,
        one_layer=one_layer,
        part=part,
        rows=rows,
    )
    deepest = max(g["count"] for g in groups)
    blocks = row_count // rows
    buffers = (
        [((ranges[i][1],) + inputs[i].shape[1:], inputs[i].dtype) for i in held]
        + [
            (shape, F32),
            ((len(places), 1, most * part), jnp.int32),
            ((len(places), most * part, col_count), BF16),
            ((len(places), most * part, col_count), BF16),
        ]
        + dense_shapes
        + [(shape, F32)] * max(len(bases) - 1, 0)
        + [((4 * part, 2 * depth), BF16)]
    )
    return pl.pallas_call(
        functools.partial(stage_kernel, plan),
        in_specs=[pl.BlockSpec(memory_space=pl.ANY if i in kept else pltpu.HBM) for i in range(len(inputs))],
        out_specs=[pl.BlockSpec(memory_space=pltpu.HBM)] * pieces + [pl.BlockSpec(memory_space=pl.ANY)] * len(dense_shapes),
        out_shape=out_shape,
        scratch_shapes=[pltpu.VMEM(dims, kind) for dims, kind in buffers]
        + [
            pltpu.SemaphoreType.DMA((len(held), deepest)),
            pltpu.SemaphoreType.DMA((max(len(bases), 1), blocks)),
            pltpu.SemaphoreType.DMA((1 + len(dense_shapes), max(blocks, total))),
        ],
        compiler_params=pltpu.CompilerParams(vmem_limit_bytes=VMEM_ALL),
        cost_estimate=pl.CostEstimate(flops=1000, bytes_accessed=1000, transcendentals=0),
    )(*inputs)


ENDS = [(0, 1), (1, 0), (2, 3), (3, 2)]
MIDDLE = [(1, 2), (2, 1)]
OUTWARD = [(1, 0), (2, 3)]
SWAP_X = [(0, 1), (1, 0), (2, 3), (3, 2)]
SWAP_Y = [(0, 2), (2, 0), (1, 3), (3, 1)]
SWAP_XY = [(0, 3), (3, 0), (1, 2), (2, 1)]


def four_by_four(front_matrix, l_panels, l_map, u_panels, u_map):
    shape = front_matrix.shape
    l_own = l_panels[0, :, 0]
    u_own = u_panels[0, :, 0]
    children = u_own.shape[0]
    first = children // 2
    late = children // 4
    rest, early = children - first, children - late
    row_map = l_map.reshape(children, 4, -1)
    col_map = u_map.reshape(children, 1, -1)
    swap = [(0, 1), (1, 0)]
    together = lax.optimization_barrier

    pair = lax.ppermute(l_own, "col", ENDS)
    mid_b = lax.ppermute(l_own, "col", MIDDLE)
    by_x = lax.ppermute(u_own, "row", SWAP_X)
    by_y = lax.ppermute(u_own, "row", SWAP_Y)
    pair, by_x, by_y = together((pair, by_x, by_y))

    def diagonal(start, count):
        cut = start + count // 2
        return (
            lax.ppermute(by_x[start:cut], "row", SWAP_Y),
            lax.ppermute(by_y[cut : start + count], "row", SWAP_X),
        )

    mid_a = lax.ppermute(mid_b, "col", OUTWARD)
    far_b = lax.ppermute(pair, "col", MIDDLE)
    by_xy1 = diagonal(0, first)
    by_xy2 = diagonal(first, rest)
    row_map_other = lax.ppermute(row_map, "gz", swap)

    def near(base, start, count, u, chunks=(), groups=(), **options):
        group = dict(
            count=count,
            map=(row_map, start),
            col_map=(col_map, start),
            u=[(u_own, start), (by_x, start), (by_y, start)] + [(x, 0) for x in u],
            cut=count // 2,
            chunks=[(0, 0, [(l_own, start)]), (1, 0, [(pair, start)]), *chunks],
        )
        places = [(0, count), (1, count)] + [(2, children)] * len(chunks)
        return stage(shape, [base], places, [group, *groups], **options)

    mine, *dense1 = near([front_matrix], 0, first, by_xy1, emit_sums=late, one_layer=True)
    dense1, sums = dense1[:2], dense1[2:]
    far_b2, far_b1 = far_b[:late], far_b[late:]
    far_b1, far_b2, mid_a, mine = together((far_b1, far_b2, mid_a, mine))
    far_a1 = lax.ppermute(far_b1, "col", OUTWARD)
    far_a2 = lax.ppermute(far_b2, "col", OUTWARD)
    far_b2_other = lax.ppermute(far_b2, "gz", swap)
    *sums, by_xy2a, by_xy2b = together((*sums, *by_xy2))
    sums_other = [lax.ppermute(x, "gz", swap) for x in sums]
    mine, *dense2 = near(
        [mine],
        first,
        rest,
        (by_xy2a, by_xy2b),
        [(2, first, [(mid_a, first), (mid_b, first)])],
        [
            dict(
                count=first,
                map=(row_map, 0),
                dense=[(d, 0) for d in dense1],
                chunks=[(2, 0, [(mid_a, 0), (mid_b, 0)])],
            )
        ],
        emit_sums=0,
    )
    mine, far_b2_other, *sums_other = together((mine, far_b2_other, *sums_other))
    top, bottom = stage(
        shape,
        [[mine]],
        [(3, early)],
        [
            dict(
                count=first - late,
                map=(row_map, late),
                dense=[(d, late) for d in dense1],
                chunks=[(0, 0, [(far_a1, 0), (far_b1, 0)])],
            ),
            dict(
                count=rest,
                map=(row_map, first),
                dense=[(d, 0) for d in dense2],
                chunks=[(0, first - late, [(far_a1, first - late), (far_b1, first - late)])],
            ),
        ],
        pieces=2,
    )
    other_top = lax.ppermute(top, "gz", swap)
    sent, far_a2 = together((bottom, far_a2))
    far_a2_other = lax.ppermute(far_a2, "gz", swap)
    other_bottom = lax.ppermute(sent, "gz", swap)
    late_groups = [
        dict(
            count=1,
            map=(slot_map, c),
            dense=[(x, 0)],
            chunks=[(0, at, [(far, c) for far in fars])],
        )
        for slot_map, denses, fars, at in (
            (row_map, sums, (far_a2, far_b2), lambda layer: layer * late),
            (row_map_other, sums_other, (far_a2_other, far_b2_other), lambda layer: (1 - layer) * late),
        )
        for c, x in enumerate(denses)
    ]
    for g in late_groups:
        place, at, fars = g["chunks"][0]
        g["chunks"] = [(place, functools.partial(lambda at, c, layer: at(layer) + c, at, g["map"][1]), fars)]
    (out,) = stage(shape, [[top, bottom], [other_top, other_bottom]], [(3, 2 * late)], late_groups)
    return out


def solution(mesh):
    placed = (
        P("row", "col"),
        P("gz", None, "row", "col", None),
        P("gz", None, "row", None),
        P("gz", None, "col", "row", None),
        P("gz", None, "col", None),
    )
    square = mesh.shape["row"] == 4 and mesh.shape["col"] == 4
    return jax.shard_map(
        four_by_four if square else any_mesh,
        mesh=mesh,
        in_specs=placed,
        out_specs=P("row", "col"),
        check_vma=False,
    )
```
